32 devices in a mesh: gx: 4 (over x, core), gy: 8 (over z, y).
Axes of the slice: x: 2, y: 2, z: 4, core: 2. Of those that a mesh axis runs over, the one named last changes fastest.
Arguments:
- old_heads: float32 [4, 512, 1024], P(None, 'gx', 'gy'), may hold values from -6 to 6
- conductance_x: float32 [4, 512, 1024], P(None, 'gx', 'gy'), may hold values from 7.6 to 10.4
- conductance_y: float32 [4, 512, 1024], P(None, 'gx', 'gy'), may hold values from 7.6 to 10.4
- storage: float32 [4, 512, 1024], P(None, 'gx', 'gy'), may hold values from 0.25 to 4
- sources: float32 [4, 512, 1024], P(None, 'gx', 'gy'), may hold values from -6 to 6
- cotangent: float32 [4, 512, 1024], P(None, 'gx', 'gy'), may hold values from -6 to 6
- active_mask: int32 [512, 1024], P('gx', 'gy'), may hold values from 0 to 1, as said below
- layer_scale: float32 [64], replicated, may hold values from 0.5 to 2
- window_layers: int32 [4], replicated, may hold values from 0 to 63
Outputs:
- new_heads: float32 [4, 512, 1024], P(None, 'gx', 'gy')
- grad_heads: float32 [4, 512, 1024], P(None, 'gx', 'gy')
- sensitivity_x: float32 [4, 512, 1024], P(None, 'gx', 'gy')
- sensitivity_y: float32 [4, 512, 1024], P(None, 'gx', 'gy')
The draws below stay inside these ranges and needn't reach their ends.
Inputs may be any that keep to these rules, and one draw needn't show every extreme that they name: `active_mask`: 1 for an active column of cells, 0 for an inactive one.
All inputs are finite; a program needn't handle non-finite values.
Results may differ from the reference program's by a relative error of at most 0.0017.
Values sent between devices are 32-bit elements; how exact they have to be, the bound alone decides.
A program may use at most 128 MiB of HBM per device.

```python
import math
import jax
import jax.numpy as jnp
from jax import lax

ALL_LAYERS = 64
LAYERS = 4
NX = 512
NY = 1024


def draw_active_mask(key, part):
    keys = jax.random.split(key, 5)
    margin_y = max(NY // 16, 1)
    margin_x = max(NX // 16, 1)
    left_edge = jax.random.randint(keys[0], (NX, 1), 1, margin_y + 1)
    right_edge = NY - jax.random.randint(keys[1], (NX, 1), 1, margin_y + 1)
    top_edge = jax.random.randint(keys[2], (1, NY), 1, margin_x + 1)
    bottom_edge = NX - jax.random.randint(keys[3], (1, NY), 1, margin_x + 1)
    row_index = jnp.arange(NX, dtype=jnp.int32)[:, None]
    col_index = jnp.arange(NY, dtype=jnp.int32)[None, :]
    inside = (col_index >= left_edge) & (col_index < right_edge) & (row_index >= top_edge) & (row_index < bottom_edge)
    wells = jax.random.randint(keys[4], (NX, NY), 0, 1024) == 0
    return jnp.where(inside & jnp.logical_not(wells), 1, 0).astype(jnp.int32)


def touch_ends(values, own_key, low, top_value):
    index_at = [jax.random.randint(jax.random.fold_in(own_key, axis), (), 0, length) for axis, length in enumerate(values.shape)]
    longest = values.shape.index(max(values.shape))
    beside = index_at[:longest] + [(index_at[longest] + 1) % values.shape[longest]] + index_at[longest + 1:]
    return values.at[tuple(index_at)].set(low).at[tuple(beside)].set(top_value)


def block_levels(rng, extent, shards, smallest, largest):
    level = 1.0
    for position, shards_of in shards:
        draws = jax.random.uniform(jax.random.fold_in(jax.random.fold_in(rng, 6), position), (shards_of,), jnp.float32, smallest / len(shards), largest / len(shards))
        level = level * jnp.repeat(jnp.exp(draws), extent[position] // shards_of).reshape((-1,) + (1,) * (len(extent) - 1 - position))
    return level


def normal_values(rng, shape, scale, most, cuts=(), kind=jnp.bfloat16):
    values = jax.random.normal(rng, shape, jnp.float32) * scale
    if len(cuts) > 0:
        values = block_levels(rng, shape, cuts, -0.22, 0.18) * values
    return jnp.clip(values, min=-most, max=most).astype(kind)


def setup_inputs(seed: int = 0) -> dict:
    seeds = jax.random.split(jax.random.key(seed), 10)
    return {
        "old_heads": normal_values(seeds[0], (LAYERS, NX, NY), 1.0, 6.0, ((1, 4), (2, 8)), jnp.float32),
        "conductance_x": jnp.clip(7.6 + 2.7999997 * jax.random.uniform(seeds[1], (LAYERS, NX, NY), jnp.float32) ** block_levels(seeds[1], (LAYERS, NX, NY), ((1, 4), (2, 8)), -0.2, 0.2), 7.6, 10.4),
        "conductance_y": jnp.clip(7.6 + 2.7999997 * jax.random.uniform(seeds[2], (LAYERS, NX, NY), jnp.float32) ** block_levels(seeds[2], (LAYERS, NX, NY), ((1, 4), (2, 8)), -0.2, 0.2), 7.6, 10.4),
        "storage": jnp.clip(jnp.exp(math.log(4.0) - 2.7725887 * jax.random.uniform(seeds[3], (LAYERS, NX, NY), jnp.float32) ** block_levels(seeds[3], (LAYERS, NX, NY), ((1, 4), (2, 8)), -0.2, 0.2)), 0.25, 4.0),
        "sources": normal_values(seeds[4], (LAYERS, NX, NY), 1.0, 6.0, ((1, 4), (2, 8)), jnp.float32),
        "cotangent": normal_values(seeds[5], (LAYERS, NX, NY), 1.0, 6.0, ((1, 4), (2, 8)), jnp.float32),
        "active_mask": draw_active_mask(jax.random.fold_in(seeds[9], 71), 0),
        "layer_scale": jnp.clip(jnp.exp(jax.random.uniform(seeds[7], (ALL_LAYERS,), jnp.float32, math.log(0.5), math.log(2.0))), 0.5, 2.0),
        "window_layers": touch_ends(jax.random.randint(seeds[8], (LAYERS,), 0, ALL_LAYERS), jax.random.fold_in(seeds[8], 1), 0, ALL_LAYERS - 1).astype(jnp.int32),
    }


def layer_weights(layer_scale, window_layers):
    matches = window_layers[:, None] == jnp.arange(layer_scale.shape[0], dtype=jnp.int32)[None, :]
    return jnp.sum(jnp.where(matches, layer_scale[None, :], jnp.float32(0.0)), axis=1)


def next_along(values, line_axis):
    length = values.shape[line_axis]
    rest = lax.slice_in_dim(values, 1, length, axis=line_axis)
    filler = jnp.zeros_like(lax.slice_in_dim(values, 0, 1, axis=line_axis))
    return jnp.concatenate([rest, filler], axis=line_axis)


def prev_along(values, line_axis):
    length = values.shape[line_axis]
    rest = lax.slice_in_dim(values, 0, length - 1, axis=line_axis)
    filler = jnp.zeros_like(lax.slice_in_dim(values, 0, 1, axis=line_axis))
    return jnp.concatenate([filler, rest], axis=line_axis)


def thomas(lower_band, diag_band, upper_band, right_side):
    zeros_row = jnp.zeros_like(right_side[0])

    def downward(state, entries):
        pivot_prev, partial_prev = state
        lower_now, diag_now, upper_now, rhs_now = entries
        denom = diag_now - lower_now * pivot_prev
        pivot_now = upper_now / denom
        partial_now = (rhs_now - lower_now * partial_prev) / denom
        return (pivot_now, partial_now), (pivot_now, partial_now)

    unused, (pivots, partials) = lax.scan(downward, (zeros_row, zeros_row), (lower_band, diag_band, upper_band, right_side))

    def upward(later, entries):
        pivot_now, partial_now = entries
        value_now = partial_now - pivot_now * later
        return value_now, value_now

    unused_last, solved = lax.scan(upward, zeros_row, (pivots, partials), reverse=True)
    return solved


def line_solve(faces, storage, right_side, line_axis):
    after = jnp.moveaxis(faces, line_axis, 0)
    store_moved = jnp.moveaxis(storage, line_axis, 0)
    rhs_moved = jnp.moveaxis(right_side, line_axis, 0)
    before = prev_along(after, 0)
    solved = thomas(-before, store_moved + before + after, -after, rhs_moved)
    return jnp.moveaxis(solved, 0, line_axis)


def reference(old_heads, conductance_x, conductance_y, storage, sources, cotangent, active_mask, layer_scale, window_layers):
    active = active_mask.astype(jnp.float32)
    weight = layer_weights(layer_scale, window_layers)[:, None, None]
    xfaces = jnp.exp(conductance_x) * weight * (active * next_along(active, 0))[None]
    yfaces = jnp.exp(conductance_y) * weight * (active * next_along(active, 1))[None]
    mid_heads = line_solve(xfaces, storage, storage * old_heads + sources, 1)
    new_heads = line_solve(yfaces, storage, storage * mid_heads, 2)
    adjoint_y = line_solve(yfaces, storage, cotangent, 2)
    adjoint_x = line_solve(xfaces, storage, storage * adjoint_y, 1)
    grad_heads = storage * adjoint_x
    sensitivity_x = -xfaces * (adjoint_x - next_along(adjoint_x, 1)) * (mid_heads - next_along(mid_heads, 1))
    sensitivity_y = -yfaces * (adjoint_y - next_along(adjoint_y, 2)) * (new_heads - next_along(new_heads, 2))
    return new_heads, grad_heads, sensitivity_x, sensitivity_y
```

```python
import functools

import jax
import jax.numpy as jnp
from jax import lax
from jax.experimental import pallas as pl
from jax.experimental.pallas import tpu as pltpu
from jax.sharding import PartitionSpec as P

MESH = pl.DeviceIdType.MESH
BLOCKS = 8
SHIFTS = (1, 2, 4)
G1, G2, T, R1, R2, F, A = range(7)


def schedule(length):
    alive = list(range(length))
    order = []
    while len(alive) > 2:
        gone = alive[1:-1:2]
        for node in gone:
            at = alive.index(node)
            order.append((node, alive[at - 1], alive[at + 1]))
        alive = [node for node in alive if node not in gone]
    return order


def weights(fl, fr, s):
    inv = 1.0 / (fl + fr + s)
    return fl * inv, fr * inv, inv


def merge(a, b, face):
    g1, g2, t = a
    bg1, bg2, bt = b
    wla, wra, ia = weights(t, face, g2)
    through = t * wra
    gb = bg1 + wra * g2
    wlb, wrb, ib = weights(through, bt, gb)
    return (g1 + wla * g2 + wlb * gb, bg2 + wrb * gb, through * wrb), (wla, wra, ia, wlb, wrb, ib)


def merge_right(a, b, coef):
    wla, wra, ia, wlb, wrb, ib = coef
    r1, r2 = a
    rb = b[0] + wra * r2
    return (r1 + wla * r2 + wlb * rb, b[1] + wrb * rb), (r2 * ia, rb * ib)


def split(x1, x2, coef, parts):
    wla, wra, _, wlb, wrb, _ = coef
    b1 = wlb * x1 + wrb * x2 + parts[1]
    a2 = wla * x1 + wra * b1 + parts[0]
    return a2, b1


def roll(value, shift):
    return pltpu.roll(value, shift % BLOCKS, 1)


def sub_index(shape):
    return lax.broadcasted_iota(jnp.int32, shape, 1)


def slab(ref, k, step):
    return ref[:, pl.ds(k, BLOCKS, stride=step), :]


def put_slab(ref, k, step, value):
    ref[:, pl.ds(k, BLOCKS, stride=step), :] = value


class Direction:
    def __init__(self, axis, count, length, layers, refs):
        self.axis, self.count, self.step, self.layers = axis, count, length // BLOCKS, layers
        (self.coef, self.part, self.face, self.flux, self.bcoef, self.bpart, self.dcoef, self.dx, self.ends,
         self.buf_a, self.buf_b, self.send_a, self.recv_a, self.send_b, self.recv_b) = refs
        self.me = lax.axis_index(axis)
        self.order = schedule(self.step)

    def peer(self, offset):
        return lax.rem(self.me + offset, self.count)

    def greet(self, barrier):
        for offset in range(1, self.count):
            pl.semaphore_signal(barrier, inc=1, device_id={self.axis: self.peer(offset)}, device_id_type=MESH)

    def copies(self, buf, send, recv):
        return [
            pltpu.make_async_remote_copy(
                src_ref=buf.at[self.me],
                dst_ref=buf.at[self.me],
                send_sem=send.at[offset - 1],
                recv_sem=recv.at[offset - 1],
                device_id={self.axis: self.peer(offset)},
                device_id_type=MESH,
            )
            for offset in range(1, self.count)
        ]

    def reduce_right(self, right, phase):
        for i, l, r in self.order:
            wl, wr, inv = self.coef[i, 0], self.coef[i, 1], self.coef[i, 2]
            right[l] = right[l] + wl * right[i]
            right[r] = right[r] + wr * right[i]
            self.part[phase, i] = right[i] * inv
        pair = (right[0], right[-1])
        for level, shift in enumerate(SHIFTS):
            coef = [self.bcoef[level, c] for c in range(6)]
            pair, parts = merge_right(pair, [roll(v, -shift) for v in pair], coef)
            self.bpart[phase, level, 0], self.bpart[phase, level, 1] = parts
        return pair

    def post(self, buf, at, value, sub=0):
        for layer in range(self.layers):
            buf[self.me, pl.ds(at * self.layers + layer, 1), :] = value[layer, sub : sub + 1, :]

    def begin_a(self, cond, storage, active, weight, right_of):
        step = self.step
        act = [active[pl.ds(k, BLOCKS, stride=step), :] for k in range(step)]
        weight = weight[...]
        store = [slab(storage, k, step) for k in range(step)]
        right = [right_of(k) for k in range(step)]
        face = []
        for k in range(step):
            raw = jnp.exp(slab(cond, k, step)) * weight * act[k][None]
            if k == step - 1:
                self.post(self.buf_a, F, raw, BLOCKS - 1)
                after = pltpu.roll(act[0], BLOCKS - 1, 0)
            else:
                after = act[k + 1]
            face.append(raw * after[None])
            self.face[k] = face[k]
        for i, l, r in self.order:
            wl, wr, inv = weights(face[l], face[i], store[i])
            store[l] = store[l] + wl * store[i]
            store[r] = store[r] + wr * store[i]
            face[l] = face[l] * wr
            self.coef[i, 0], self.coef[i, 1], self.coef[i, 2] = wl, wr, inv
        seg, link = (store[0], store[-1], face[0]), face[-1]
        for level, shift in enumerate(SHIFTS):
            seg, coef = merge(seg, [roll(v, -shift) for v in seg], link)
            link = roll(link, -shift)
            for c in range(6):
                self.bcoef[level, c] = coef[c]
        pair = self.reduce_right(right, 0)
        for at, value in ((G1, seg[0]), (G2, seg[1]), (T, seg[2]), (R1, pair[0]), (R2, pair[1])):
            self.post(self.buf_a, at, value)
        rows = self.layers * A
        self.buf_a[self.me, pl.ds(rows, 8), :] = jnp.broadcast_to(act[0][0:1], (8, act[0].shape[1]))

    def begin_b(self, right_of):
        pair = self.reduce_right([right_of(k) for k in range(self.step)], 1)
        self.post(self.buf_b, 0, pair[0])
        self.post(self.buf_b, 1, pair[1])

    def dev(self, d, at):
        return self.buf_a[d, pl.ds(at * self.layers, self.layers), :]

    def factor_devices(self):
        first_act = [self.buf_a[d, pl.ds(self.layers * A, 1), :] for d in range(self.count)]
        segs = [tuple(self.dev(d, q) for q in (G1, G2, T)) for d in range(self.count)]
        faces = [self.dev(d, F) * first_act[d + 1] for d in range(self.count - 1)] + [jnp.zeros_like(segs[0][0])]
        for d in range(self.count):
            self.ends[d, pl.ds(0, self.layers), :] = faces[d]
        slot = 0
        while len(segs) > 1:
            joined, links = [], []
            for at in range(0, len(segs) - 1, 2):
                seg, coef = merge(segs[at], segs[at + 1], faces[at])
                for c in range(6):
                    self.dcoef[slot, c] = coef[c]
                slot += 1
                joined.append(seg)
                links.append(faces[at + 1])
            if len(segs) % 2:
                joined.append(segs[-1])
                links.append(faces[-1])
            segs, faces = joined, links
        g1, g2, t = segs[0]
        inv = 1.0 / (t + g2)
        w = t * inv
        self.dcoef[slot, 0], self.dcoef[slot, 1], self.dcoef[slot, 2] = w, inv, 1.0 / (g1 + w * g2)

    def solve_devices(self, pairs):
        slot, tree = 0, []
        while len(pairs) > 1:
            joined, record = [], []
            for at in range(0, len(pairs) - 1, 2):
                coef = [self.dcoef[slot, c] for c in range(6)]
                pair, parts = merge_right(pairs[at], pairs[at + 1], coef)
                slot += 1
                joined.append(pair)
                record.append((coef, parts))
            if len(pairs) % 2:
                joined.append(pairs[-1])
                record.append(None)
            pairs = joined
            tree.append(record)
        r1, r2 = pairs[0]
        w, inv, top = (self.dcoef[slot, c] for c in range(3))
        x1 = (r1 + w * r2) * top
        found = [(x1, w * x1 + r2 * inv)]
        for record in reversed(tree):
            lower = []
            for (x1, x2), entry in zip(found, record):
                if entry is None:
                    lower.append((x1, x2))
                else:
                    a2, b1 = split(x1, x2, *entry)
                    lower += [(x1, a2), (b1, x2)]
            found = lower
        for d, (x1, x2) in enumerate(found):
            self.dx[d, pl.ds(0, self.layers), :] = x1
            self.dx[d, pl.ds(self.layers, self.layers), :] = x2

    def wide(self, ref, index, row):
        rows = [ref[index, pl.ds(row + layer, 1), :] for layer in range(self.layers)]
        return jnp.stack([jnp.broadcast_to(v, (BLOCKS, v.shape[1])) for v in rows])

    def expand(self, phase):
        first, last = self.wide(self.dx, self.me, 0), self.wide(self.dx, self.me, self.layers)
        beyond = self.wide(self.dx, jnp.minimum(self.me + 1, self.count - 1), 0)
        block = sub_index(first.shape)
        for level in reversed(range(len(SHIFTS))):
            shift = SHIFTS[level]
            coef = [self.bcoef[level, c] for c in range(6)]
            a2, b1 = split(first, last, coef, (self.bpart[phase, level, 0], self.bpart[phase, level, 1]))
            odd = lax.rem(block, 2 * shift) == shift
            first = jnp.where(odd, roll(b1, shift), first)
            last = jnp.where(odd, roll(last, shift), a2)
        x = [None] * self.step
        x[0], x[-1] = first, last
        for i, l, r in reversed(self.order):
            x[i] = self.coef[i, 0] * x[l] + self.coef[i, 1] * x[r] + self.part[phase, i]
        after = x[1:] + [jnp.where(block == BLOCKS - 1, beyond, roll(x[0], -1))]
        return x, [now - then for now, then in zip(x, after)]

    def end_a(self):
        self.factor_devices()
        self.solve_devices([(self.dev(d, R1), self.dev(d, R2)) for d in range(self.count)])
        x, change = self.expand(0)
        for k in range(self.step):
            face = self.face[k]
            if k == self.step - 1:
                face = jnp.where(sub_index(face.shape) == BLOCKS - 1, self.wide(self.ends, self.me, 0), face)
            self.flux[k] = -face * change[k]
        return x

    def end_b(self):
        n = self.layers
        self.solve_devices([(self.buf_b[d, pl.ds(0, n), :], self.buf_b[d, pl.ds(n, n), :]) for d in range(self.count)])
        x, change = self.expand(1)
        return x, [self.flux[k] * change[k] for k in range(self.step)]


def kernel(counts, heads, cond_x, cond_y, storage, sources, cotangent, mask, scale, window,
           new_heads, grad_heads, sens_x, sens_y,
           weight, act, act_t, cond_t, store_t, work, work_t, other_t, *rest):
    layers, rows, columns = heads.shape
    half = len(rest) // 2
    x = Direction("gx", counts[0], rows, layers, rest[:half])
    y = Direction("gy", counts[1], columns, layers, rest[half:])
    barrier = pltpu.get_barrier_semaphore()
    x.greet(barrier)
    y.greet(barrier)

    for layer in range(layers):
        weight[layer] = jnp.full(weight.shape[1:], scale[window[layer]], jnp.float32)
    act[...] = mask[...].astype(jnp.float32)
    act_t[...] = act[...].T
    for layer in range(layers):
        cond_t[layer] = cond_y[layer].T
        store_t[layer] = storage[layer].T
        work_t[layer] = cotangent[layer].T

    y.begin_a(cond_t, store_t, act_t, weight, lambda k: slab(work_t, k, y.step))
    pl.semaphore_wait(barrier, counts[0] + counts[1] - 2)
    y_a = y.copies(y.buf_a, y.send_a, y.recv_a)
    for copy in y_a:
        copy.start()

    x.begin_a(cond_x, storage, act, weight,
              lambda k: slab(storage, k, x.step) * slab(heads, k, x.step) + slab(sources, k, x.step))
    x_a = x.copies(x.buf_a, x.send_a, x.recv_a)
    for copy in x_a:
        copy.start()

    for copy in x_a:
        copy.wait()
    for k, value in enumerate(x.end_a()):
        put_slab(work, k, x.step, slab(storage, k, x.step) * value)
    for layer in range(layers):
        work_t[layer] = work[layer].T
    y.begin_b(lambda k: slab(work_t, k, y.step))

    for copy in y_a:
        copy.wait()
    y_b = y.copies(y.buf_b, y.send_b, y.recv_b)
    for copy in y_b:
        copy.start()
    for k, value in enumerate(y.end_a()):
        put_slab(other_t, k, y.step, slab(store_t, k, y.step) * value)
    for layer in range(layers):
        work[layer] = other_t[layer].T
    x.begin_b(lambda k: slab(work, k, x.step))
    x_b = x.copies(x.buf_b, x.send_b, x.recv_b)
    for copy in x_b:
        copy.start()

    for copy in y_b:
        copy.wait()
    values, sens = y.end_b()
    for k in range(y.step):
        put_slab(work_t, k, y.step, values[k])
        put_slab(other_t, k, y.step, sens[k])
    for layer in range(layers):
        new_heads[layer] = work_t[layer].T
        sens_y[layer] = other_t[layer].T

    for copy in x_b:
        copy.wait()
    values, sens = x.end_b()
    for k in range(x.step):
        put_slab(grad_heads, k, x.step, slab(storage, k, x.step) * values[k])
        put_slab(sens_x, k, x.step, sens[k])


def direction_scratch(count, length, width, layers):
    step = length // BLOCKS
    tile = (layers, BLOCKS, width)
    rows_a = -(-(layers * A + 8) // 8) * 8
    rows_b = -(-(layers * 2) // 8) * 8
    sems = pltpu.SemaphoreType.DMA((max(count - 1, 1),))
    return [
        pltpu.VMEM((step, 3) + tile, jnp.float32),
        pltpu.VMEM((2, step) + tile, jnp.float32),
        pltpu.VMEM((step,) + tile, jnp.float32),
        pltpu.VMEM((step,) + tile, jnp.float32),
        pltpu.VMEM((len(SHIFTS), 6) + tile, jnp.float32),
        pltpu.VMEM((2, len(SHIFTS), 2) + tile, jnp.float32),
        pltpu.VMEM((count, 6, layers, width), jnp.float32),
        pltpu.VMEM((count, rows_b, width), jnp.float32),
        pltpu.VMEM((count, rows_b, width), jnp.float32),
        pltpu.VMEM((count, rows_a, width), jnp.float32),
        pltpu.VMEM((count, rows_b, width), jnp.float32),
        sems, sems, sems, sems,
    ]


def solution(mesh):
    counts = (mesh.shape["gx"], mesh.shape["gy"])

    def on_device(*args):
        layers, rows, columns = args[0].shape
        vmem = pl.BlockSpec(memory_space=pltpu.VMEM)
        smem = pl.BlockSpec(memory_space=pltpu.SMEM)
        natural = pltpu.VMEM((layers, rows, columns), jnp.float32)
        turned = pltpu.VMEM((layers, columns, rows), jnp.float32)
        return pl.pallas_call(
            functools.partial(kernel, counts),
            out_shape=[jax.ShapeDtypeStruct(args[0].shape, jnp.float32)] * 4,
            in_specs=[vmem] * 7 + [smem] * 2,
            out_specs=[vmem] * 4,
            scratch_shapes=[
                pltpu.VMEM((layers, BLOCKS, columns), jnp.float32),
                pltpu.VMEM((rows, columns), jnp.float32),
                pltpu.VMEM((columns, rows), jnp.float32),
                turned, turned, natural, turned, turned,
            ]
            + direction_scratch(counts[0], rows, columns, layers)
            + direction_scratch(counts[1], columns, rows, layers),
            compiler_params=pltpu.CompilerParams(
                collective_id=0, has_side_effects=True, vmem_limit_bytes=40 * 2**20
            ),
        )(*args)

    block = P(None, "gx", "gy")
    return jax.shard_map(
        on_device,
        mesh=mesh,
        in_specs=(block,) * 6 + (P("gx", "gy"), P(), P()),
        out_specs=(block,) * 4,
        check_vma=False,
    )
```

```python
import functools

import jax
import jax.numpy as jnp
from jax import lax
from jax.experimental import pallas as pl
from jax.experimental.pallas import tpu as pltpu
from jax.sharding import PartitionSpec as P

MESH = pl.DeviceIdType.MESH
BLOCKS = 8
SHIFTS = (1, 2, 4)
G1, G2, T, R1, R2, F, A = range(7)


def schedule(length):
    alive = list(range(length))
    order = []
    while len(alive) > 2:
        gone = alive[1:-1:2]
        for node in gone:
            at = alive.index(node)
            order.append((node, alive[at - 1], alive[at + 1]))
        alive = [node for node in alive if node not in gone]
    return order


def weights(fl, fr, s):
    inv = 1.0 / (fl + fr + s)
    return fl * inv, fr * inv, inv


def merge(a, b, face):
    g1, g2, t = a
    bg1, bg2, bt = b
    wla, wra, ia = weights(t, face, g2)
    through = t * wra
    gb = bg1 + wra * g2
    wlb, wrb, ib = weights(through, bt, gb)
    return (g1 + wla * g2 + wlb * gb, bg2 + wrb * gb, through * wrb), (wla, wra, ia, wlb, wrb, ib)


def merge_right(a, b, coef):
    wla, wra, ia, wlb, wrb, ib = coef
    r1, r2 = a
    rb = b[0] + wra * r2
    return (r1 + wla * r2 + wlb * rb, b[1] + wrb * rb), (r2 * ia, rb * ib)


def split(x1, x2, coef, parts):
    wla, wra, _, wlb, wrb, _ = coef
    b1 = wlb * x1 + wrb * x2 + parts[1]
    a2 = wla * x1 + wra * b1 + parts[0]
    return a2, b1


def roll(value, shift):
    return pltpu.roll(value, shift % BLOCKS, 1)


def sub_index(shape):
    return lax.broadcasted_iota(jnp.int32, shape, 1)


def slab(ref, k, step):
    return ref[:, pl.ds(k, BLOCKS, stride=step), :]


def put_slab(ref, k, step, value):
    ref[:, pl.ds(k, BLOCKS, stride=step), :] = value


class Direction:
    def __init__(self, axis, count, length, layers, refs):
        self.axis, self.count, self.step, self.layers = axis, count, length // BLOCKS, layers
        (self.coef, self.part, self.face, self.flux, self.bcoef, self.bpart, self.dcoef, self.dx, self.ends,
         self.buf_a, self.buf_b, self.send_a, self.recv_a, self.send_b, self.recv_b) = refs
        self.me = lax.axis_index(axis)
        self.order = schedule(self.step)

    def peer(self, offset):
        return lax.rem(self.me + offset, self.count)

    def greet(self, barrier):
        for offset in range(1, self.count):
            pl.semaphore_signal(barrier, inc=1, device_id={self.axis: self.peer(offset)}, device_id_type=MESH)

    def copies(self, buf, send, recv):
        return [
            pltpu.make_async_remote_copy(
                src_ref=buf.at[self.me],
                dst_ref=buf.at[self.me],
                send_sem=send.at[offset - 1],
                recv_sem=recv.at[offset - 1],
                device_id={self.axis: self.peer(offset)},
                device_id_type=MESH,
            )
            for offset in range(1, self.count)
        ]

    def reduce_right(self, right, phase):
        for i, l, r in self.order:
            wl, wr, inv = self.coef[i, 0], self.coef[i, 1], self.coef[i, 2]
            right[l] = right[l] + wl * right[i]
            right[r] = right[r] + wr * right[i]
            self.part[phase, i] = right[i] * inv
        pair = (right[0], right[-1])
        for level, shift in enumerate(SHIFTS):
            coef = [self.bcoef[level, c] for c in range(6)]
            pair, parts = merge_right(pair, [roll(v, -shift) for v in pair], coef)
            self.bpart[phase, level, 0], self.bpart[phase, level, 1] = parts
        return pair

    def post(self, buf, at, value, sub=0):
        for layer in range(self.layers):
            buf[self.me, pl.ds(at * self.layers + layer, 1), :] = value[layer, sub : sub + 1, :]

    def begin_a(self, cond, storage, active, weight, right_of):
        step = self.step
        act = [active[pl.ds(k, BLOCKS, stride=step), :] for k in range(step)]
        weight = weight[...]
        store = [slab(storage, k, step) for k in range(step)]
        right = [right_of(k) for k in range(step)]
        face = []
        for k in range(step):
            raw = jnp.exp(slab(cond, k, step)) * weight * act[k][None]
            if k == step - 1:
                self.post(self.buf_a, F, raw, BLOCKS - 1)
                after = pltpu.roll(act[0], BLOCKS - 1, 0)
            else:
                after = act[k + 1]
            face.append(raw * after[None])
            self.face[k] = face[k]
        for i, l, r in self.order:
            wl, wr, inv = weights(face[l], face[i], store[i])
            store[l] = store[l] + wl * store[i]
            store[r] = store[r] + wr * store[i]
            face[l] = face[l] * wr
            self.coef[i, 0], self.coef[i, 1], self.coef[i, 2] = wl, wr, inv
        seg, link = (store[0], store[-1], face[0]), face[-1]
        for level, shift in enumerate(SHIFTS):
            seg, coef = merge(seg, [roll(v, -shift) for v in seg], link)
            link = roll(link, -shift)
            for c in range(6):
                self.bcoef[level, c] = coef[c]
        pair = self.reduce_right(right, 0)
        for at, value in ((G1, seg[0]), (G2, seg[1]), (T, seg[2]), (R1, pair[0]), (R2, pair[1])):
            self.post(self.buf_a, at, value)
        rows = self.layers * A
        self.buf_a[self.me, pl.ds(rows, 8), :] = jnp.broadcast_to(act[0][0:1], (8, act[0].shape[1]))

    def begin_b(self, right_of):
        pair = self.reduce_right([right_of(k) for k in range(self.step)], 1)
        self.post(self.buf_b, 0, pair[0])
        self.post(self.buf_b, 1, pair[1])

    def dev(self, d, at):
        return self.buf_a[d, pl.ds(at * self.layers, self.layers), :]

    def factor_devices(self):
        first_act = [self.buf_a[d, pl.ds(self.layers * A, 1), :] for d in range(self.count)]
        segs = [tuple(self.dev(d, q) for q in (G1, G2, T)) for d in range(self.count)]
        faces = [self.dev(d, F) * first_act[d + 1] for d in range(self.count - 1)] + [jnp.zeros_like(segs[0][0])]
        for d in range(self.count):
            self.ends[d, pl.ds(0, self.layers), :] = faces[d]
        slot = 0
        while len(segs) > 1:
            joined, links = [], []
            for at in range(0, len(segs) - 1, 2):
                seg, coef = merge(segs[at], segs[at + 1], faces[at])
                for c in range(6):
                    self.dcoef[slot, c] = coef[c]
                slot += 1
                joined.append(seg)
                links.append(faces[at + 1])
            if len(segs) % 2:
                joined.append(segs[-1])
                links.append(faces[-1])
            segs, faces = joined, links
        g1, g2, t = segs[0]
        inv = 1.0 / (t + g2)
        w = t * inv
        self.dcoef[slot, 0], self.dcoef[slot, 1], self.dcoef[slot, 2] = w, inv, 1.0 / (g1 + w * g2)

    def solve_devices(self, pairs):
        slot, tree = 0, []
        while len(pairs) > 1:
            joined, record = [], []
            for at in range(0, len(pairs) - 1, 2):
                coef = [self.dcoef[slot, c] for c in range(6)]
                pair, parts = merge_right(pairs[at], pairs[at + 1], coef)
                slot += 1
                joined.append(pair)
                record.append((coef, parts))
            if len(pairs) % 2:
                joined.append(pairs[-1])
                record.append(None)
            pairs = joined
            tree.append(record)
        r1, r2 = pairs[0]
        w, inv, top = (self.dcoef[slot, c] for c in range(3))
        x1 = (r1 + w * r2) * top
        found = [(x1, w * x1 + r2 * inv)]
        for record in reversed(tree):
            lower = []
            for (x1, x2), entry in zip(found, record):
                if entry is None:
                    lower.append((x1, x2))
                else:
                    a2, b1 = split(x1, x2, *entry)
                    lower += [(x1, a2), (b1, x2)]
            found = lower
        for d, (x1, x2) in enumerate(found):
            self.dx[d, pl.ds(0, self.layers), :] = x1
            self.dx[d, pl.ds(self.layers, self.layers), :] = x2

    def wide(self, ref, index, row):
        rows = [ref[index, pl.ds(row + layer, 1), :] for layer in range(self.layers)]
        return jnp.stack([jnp.broadcast_to(v, (BLOCKS, v.shape[1])) for v in rows])

    def expand(self, phase):
        first, last = self.wide(self.dx, self.me, 0), self.wide(self.dx, self.me, self.layers)
        beyond = self.wide(self.dx, jnp.minimum(self.me + 1, self.count - 1), 0)
        block = sub_index(first.shape)
        for level in reversed(range(len(SHIFTS))):
            shift = SHIFTS[level]
            coef = [self.bcoef[level, c] for c in range(6)]
            a2, b1 = split(first, last, coef, (self.bpart[phase, level, 0], self.bpart[phase, level, 1]))
            odd = lax.rem(block, 2 * shift) == shift
            first = jnp.where(odd, roll(b1, shift), first)
            last = jnp.where(odd, roll(last, shift), a2)
        x = [None] * self.step
        x[0], x[-1] = first, last
        for i, l, r in reversed(self.order):
            x[i] = self.coef[i, 0] * x[l] + self.coef[i, 1] * x[r] + self.part[phase, i]
        after = x[1:] + [jnp.where(block == BLOCKS - 1, beyond, roll(x[0], -1))]
        return x, [now - then for now, then in zip(x, after)]

    def end_a(self):
        self.factor_devices()
        self.solve_devices([(self.dev(d, R1), self.dev(d, R2)) for d in range(self.count)])
        x, change = self.expand(0)
        for k in range(self.step):
            face = self.face[k]
            if k == self.step - 1:
                face = jnp.where(sub_index(face.shape) == BLOCKS - 1, self.wide(self.ends, self.me, 0), face)
            self.flux[k] = -face * change[k]
        return x

    def end_b(self):
        n = self.layers
        self.solve_devices([(self.buf_b[d, pl.ds(0, n), :], self.buf_b[d, pl.ds(n, n), :]) for d in range(self.count)])
        x, change = self.expand(1)
        return x, [self.flux[k] * change[k] for k in range(self.step)]


def kernel(counts, *refs):
    sources_hbm, refs = refs[:9], refs[9:]
    results, refs = refs[:4], refs[4:]
    (new_heads, grad_heads, sens_x, sens_y), leave, refs = refs[:4], refs[4], refs[5:]
    stores = [
        pltpu.make_async_copy(src, dst, leave.at[at])
        for at, (src, dst) in enumerate(zip((new_heads, grad_heads, sens_x, sens_y), results))
    ]
    copied, refs = refs[:9], refs[9:]
    heads, cond_x, cond_y, storage, sources, cotangent, mask, scale, window = copied
    (arrive, weight, act, act_t, cond_t, store_t, work, work_t, other_t), rest = refs[:9], refs[9:]
    layers, rows, columns = heads.shape
    half = len(rest) // 2
    x = Direction("gx", counts[0], rows, layers, rest[:half])
    y = Direction("gy", counts[1], columns, layers, rest[half:])
    barrier = pltpu.get_barrier_semaphore()
    x.greet(barrier)
    y.greet(barrier)
    loads = [pltpu.make_async_copy(src, dst, arrive.at[at]) for at, (src, dst) in enumerate(zip(sources_hbm, copied))]
    for at in (8, 7, 6, 1, 3, 0, 4, 2, 5):
        loads[at].start()

    loads[8].wait()
    loads[7].wait()
    for layer in range(layers):
        weight[layer] = jnp.full(weight.shape[1:], scale[window[layer]], jnp.float32)
    loads[6].wait()
    act[...] = mask[...].astype(jnp.float32)
    act_t[...] = act[...].T
    for at in (1, 3, 0, 4):
        loads[at].wait()

    x.begin_a(cond_x, storage, act, weight,
              lambda k: slab(storage, k, x.step) * slab(heads, k, x.step) + slab(sources, k, x.step))
    pl.semaphore_wait(barrier, counts[0] + counts[1] - 2)
    x_a = x.copies(x.buf_a, x.send_a, x.recv_a)
    for copy in x_a:
        copy.start()

    loads[2].wait()
    loads[5].wait()
    for layer in range(layers):
        cond_t[layer] = cond_y[layer].T
        store_t[layer] = storage[layer].T
        work_t[layer] = cotangent[layer].T
    y.begin_a(cond_t, store_t, act_t, weight, lambda k: slab(work_t, k, y.step))
    y_a = y.copies(y.buf_a, y.send_a, y.recv_a)
    for copy in y_a:
        copy.start()

    for copy in x_a:
        copy.wait()
    for k, value in enumerate(x.end_a()):
        put_slab(work, k, x.step, slab(storage, k, x.step) * value)
    for layer in range(layers):
        work_t[layer] = work[layer].T
    y.begin_b(lambda k: slab(work_t, k, y.step))
    y_b = y.copies(y.buf_b, y.send_b, y.recv_b)
    for copy in y_b:
        copy.start()

    for copy in y_a:
        copy.wait()
    for k, value in enumerate(y.end_a()):
        put_slab(other_t, k, y.step, slab(store_t, k, y.step) * value)
    for layer in range(layers):
        work[layer] = other_t[layer].T
    x.begin_b(lambda k: slab(work, k, x.step))
    x_b = x.copies(x.buf_b, x.send_b, x.recv_b)
    for copy in x_b:
        copy.start()

    for copy in y_b:
        copy.wait()
    values, sens = y.end_b()
    for k in range(y.step):
        put_slab(work_t, k, y.step, values[k])
        put_slab(other_t, k, y.step, sens[k])
    for layer in range(layers):
        new_heads[layer] = work_t[layer].T
        sens_y[layer] = other_t[layer].T
    stores[0].start()
    stores[3].start()

    for copy in x_b:
        copy.wait()
    values, sens = x.end_b()
    for k in range(x.step):
        put_slab(grad_heads, k, x.step, slab(storage, k, x.step) * values[k])
        put_slab(sens_x, k, x.step, sens[k])
    stores[1].start()
    stores[2].start()
    for copy in stores:
        copy.wait()


def write_out(*refs):
    count = len(refs) // 2
    copies = [pltpu.make_async_copy(refs[i], refs[count + i], refs[-1].at[i]) for i in range(count)]
    for copy in copies:
        copy.start()
    for copy in copies:
        copy.wait()


def direction_scratch(count, length, width, layers):
    step = length // BLOCKS
    tile = (layers, BLOCKS, width)
    rows_a = -(-(layers * A + 8) // 8) * 8
    rows_b = -(-(layers * 2) // 8) * 8
    sems = pltpu.SemaphoreType.DMA((max(count - 1, 1),))
    return [
        pltpu.VMEM((step, 3) + tile, jnp.float32),
        pltpu.VMEM((2, step) + tile, jnp.float32),
        pltpu.VMEM((step,) + tile, jnp.float32),
        pltpu.VMEM((step,) + tile, jnp.float32),
        pltpu.VMEM((len(SHIFTS), 6) + tile, jnp.float32),
        pltpu.VMEM((2, len(SHIFTS), 2) + tile, jnp.float32),
        pltpu.VMEM((count, 6, layers, width), jnp.float32),
        pltpu.VMEM((count, rows_b, width), jnp.float32),
        pltpu.VMEM((count, rows_b, width), jnp.float32),
        pltpu.VMEM((count, rows_a, width), jnp.float32),
        pltpu.VMEM((count, rows_b, width), jnp.float32),
        sems, sems, sems, sems,
    ]


def solution(mesh):
    counts = (mesh.shape["gx"], mesh.shape["gy"])

    def on_device(*args):
        layers, rows, columns = args[0].shape
        hbm = pl.BlockSpec(memory_space=pltpu.HBM)
        natural = pltpu.VMEM((layers, rows, columns), jnp.float32)
        turned = pltpu.VMEM((layers, columns, rows), jnp.float32)
        results = [jax.ShapeDtypeStruct(args[0].shape, jnp.float32)] * 4
        found = pl.pallas_call(
            functools.partial(kernel, counts),
            out_shape=results,
            in_specs=[hbm] * 9,
            out_specs=[hbm] * 4,
            scratch_shapes=[natural] * 4
            + [pltpu.SemaphoreType.DMA((4,))]
            + [pltpu.VMEM(v.shape, v.dtype) for v in args[:7]]
            + [pltpu.SMEM(v.shape, v.dtype) for v in args[7:]]
            + [
                pltpu.SemaphoreType.DMA((9,)),
                pltpu.VMEM((layers, BLOCKS, columns), jnp.float32),
                pltpu.VMEM((rows, columns), jnp.float32),
                pltpu.VMEM((columns, rows), jnp.float32),
                turned, turned, natural, turned, turned,
            ]
            + direction_scratch(counts[0], rows, columns, layers)
            + direction_scratch(counts[1], columns, rows, layers),
            compiler_params=pltpu.CompilerParams(
                collective_id=0, has_side_effects=True, vmem_limit_bytes=64 * 2**20
            ),
        )(*args)
        return pl.pallas_call(
            write_out,
            out_shape=results,
            in_specs=[hbm] * 4,
            out_specs=[hbm] * 4,
            scratch_shapes=[pltpu.SemaphoreType.DMA((4,))],
            compiler_params=pltpu.CompilerParams(vmem_limit_bytes=64 * 2**20),
        )(*found)

    block = P(None, "gx", "gy")
    return jax.shard_map(
        on_device,
        mesh=mesh,
        in_specs=(block,) * 6 + (P("gx", "gy"), P(), P()),
        out_specs=(block,) * 4,
        check_vma=False,
    )
```

```python
import functools

import jax
import jax.numpy as jnp
from jax import lax
from jax.experimental import pallas as pl
from jax.experimental.pallas import tpu as pltpu
from jax.sharding import PartitionSpec as P

MESH = pl.DeviceIdType.MESH
BLOCKS = 8
SHIFTS = (1, 2, 4)
G1, G2, T, R1, R2, F, A = range(7)


def schedule(length):
    alive = list(range(length))
    order = []
    while len(alive) > 2:
        gone = alive[1:-1:2]
        for node in gone:
            at = alive.index(node)
            order.append((node, alive[at - 1], alive[at + 1]))
        alive = [node for node in alive if node not in gone]
    return order


def weights(fl, fr, s):
    inv = 1.0 / (fl + fr + s)
    return fl * inv, fr * inv, inv


def merge(a, b, face):
    g1, g2, t = a
    bg1, bg2, bt = b
    wla, wra, ia = weights(t, face, g2)
    through = t * wra
    gb = bg1 + wra * g2
    wlb, wrb, ib = weights(through, bt, gb)
    return (g1 + wla * g2 + wlb * gb, bg2 + wrb * gb, through * wrb), (wla, wra, ia, wlb, wrb, ib)


def merge_right(a, b, coef):
    wla, wra, ia, wlb, wrb, ib = coef
    r1, r2 = a
    rb = b[0] + wra * r2
    return (r1 + wla * r2 + wlb * rb, b[1] + wrb * rb), (r2 * ia, rb * ib)


def split(x1, x2, coef, parts):
    wla, wra, _, wlb, wrb, _ = coef
    b1 = wlb * x1 + wrb * x2 + parts[1]
    a2 = wla * x1 + wra * b1 + parts[0]
    return a2, b1


def roll(value, shift):
    return pltpu.roll(value, shift % BLOCKS, 1)


def sub_index(shape):
    return lax.broadcasted_iota(jnp.int32, shape, 1)


def slab(ref, k, step):
    return ref[:, pl.ds(k, BLOCKS, stride=step), :]


def put_slab(ref, k, step, value):
    ref[:, pl.ds(k, BLOCKS, stride=step), :] = value


class Direction:
    def __init__(self, axis, count, length, layers, refs):
        self.axis, self.count, self.step, self.layers = axis, count, length // BLOCKS, layers
        (self.coef, self.part, self.face, self.flux, self.bcoef, self.bpart, self.dcoef, self.dx, self.ends,
         self.buf_a, self.buf_b, self.send_a, self.recv_a, self.send_b, self.recv_b) = refs
        self.me = lax.axis_index(axis)
        self.order = schedule(self.step)

    def peer(self, offset):
        return lax.rem(self.me + offset, self.count)

    def greet(self, barrier):
        for offset in range(1, self.count):
            pl.semaphore_signal(barrier, inc=1, device_id={self.axis: self.peer(offset)}, device_id_type=MESH)

    def copies(self, buf, send, recv):
        return [
            pltpu.make_async_remote_copy(
                src_ref=buf.at[self.me],
                dst_ref=buf.at[self.me],
                send_sem=send.at[offset - 1],
                recv_sem=recv.at[offset - 1],
                device_id={self.axis: self.peer(offset)},
                device_id_type=MESH,
            )
            for offset in range(1, self.count)
        ]

    def reduce_right(self, right, phase):
        for i, l, r in self.order:
            wl, wr, inv = self.coef[i, 0], self.coef[i, 1], self.coef[i, 2]
            right[l] = right[l] + wl * right[i]
            right[r] = right[r] + wr * right[i]
            self.part[phase, i] = right[i] * inv
        pair = (right[0], right[-1])
        for level, shift in enumerate(SHIFTS):
            coef = [self.bcoef[level, c] for c in range(6)]
            pair, parts = merge_right(pair, [roll(v, -shift) for v in pair], coef)
            self.bpart[phase, level, 0], self.bpart[phase, level, 1] = parts
        return pair

    def post(self, buf, at, value, sub=0):
        for layer in range(self.layers):
            buf[self.me, pl.ds(at * self.layers + layer, 1), :] = value[layer, sub : sub + 1, :]

    def begin_a(self, cond, storage, active, weight, right_of):
        step = self.step
        act = [active[pl.ds(k, BLOCKS, stride=step), :] for k in range(step)]
        weight = weight[...]
        store = [slab(storage, k, step) for k in range(step)]
        right = [right_of(k) for k in range(step)]
        face = []
        for k in range(step):
            raw = jnp.exp(slab(cond, k, step)) * weight * act[k][None]
            if k == step - 1:
                self.post(self.buf_a, F, raw, BLOCKS - 1)
                after = pltpu.roll(act[0], BLOCKS - 1, 0)
            else:
                after = act[k + 1]
            face.append(raw * after[None])
            self.face[k] = face[k]
        for i, l, r in self.order:
            wl, wr, inv = weights(face[l], face[i], store[i])
            store[l] = store[l] + wl * store[i]
            store[r] = store[r] + wr * store[i]
            face[l] = face[l] * wr
            self.coef[i, 0], self.coef[i, 1], self.coef[i, 2] = wl, wr, inv
        seg, link = (store[0], store[-1], face[0]), face[-1]
        for level, shift in enumerate(SHIFTS):
            seg, coef = merge(seg, [roll(v, -shift) for v in seg], link)
            link = roll(link, -shift)
            for c in range(6):
                self.bcoef[level, c] = coef[c]
        pair = self.reduce_right(right, 0)
        for at, value in ((G1, seg[0]), (G2, seg[1]), (T, seg[2]), (R1, pair[0]), (R2, pair[1])):
            self.post(self.buf_a, at, value)
        rows = self.layers * A
        self.buf_a[self.me, pl.ds(rows, 8), :] = jnp.broadcast_to(act[0][0:1], (8, act[0].shape[1]))

    def begin_b(self, right_of):
        pair = self.reduce_right([right_of(k) for k in range(self.step)], 1)
        self.post(self.buf_b, 0, pair[0])
        self.post(self.buf_b, 1, pair[1])

    def dev(self, d, at):
        return self.buf_a[d, pl.ds(at * self.layers, self.layers), :]

    def factor_devices(self):
        first_act = [self.buf_a[d, pl.ds(self.layers * A, 1), :] for d in range(self.count)]
        segs = [tuple(self.dev(d, q) for q in (G1, G2, T)) for d in range(self.count)]
        faces = [self.dev(d, F) * first_act[d + 1] for d in range(self.count - 1)] + [jnp.zeros_like(segs[0][0])]
        for d in range(self.count):
            self.ends[d, pl.ds(0, self.layers), :] = faces[d]
        slot = 0
        while len(segs) > 1:
            joined, links = [], []
            for at in range(0, len(segs) - 1, 2):
                seg, coef = merge(segs[at], segs[at + 1], faces[at])
                for c in range(6):
                    self.dcoef[slot, c] = coef[c]
                slot += 1
                joined.append(seg)
                links.append(faces[at + 1])
            if len(segs) % 2:
                joined.append(segs[-1])
                links.append(faces[-1])
            segs, faces = joined, links
        g1, g2, t = segs[0]
        inv = 1.0 / (t + g2)
        w = t * inv
        self.dcoef[slot, 0], self.dcoef[slot, 1], self.dcoef[slot, 2] = w, inv, 1.0 / (g1 + w * g2)

    def solve_devices(self, pairs):
        slot, tree = 0, []
        while len(pairs) > 1:
            joined, record = [], []
            for at in range(0, len(pairs) - 1, 2):
                coef = [self.dcoef[slot, c] for c in range(6)]
                pair, parts = merge_right(pairs[at], pairs[at + 1], coef)
                slot += 1
                joined.append(pair)
                record.append((coef, parts))
            if len(pairs) % 2:
                joined.append(pairs[-1])
                record.append(None)
            pairs = joined
            tree.append(record)
        r1, r2 = pairs[0]
        w, inv, top = (self.dcoef[slot, c] for c in range(3))
        x1 = (r1 + w * r2) * top
        found = [(x1, w * x1 + r2 * inv)]
        for record in reversed(tree):
            lower = []
            for (x1, x2), entry in zip(found, record):
                if entry is None:
                    lower.append((x1, x2))
                else:
                    a2, b1 = split(x1, x2, *entry)
                    lower += [(x1, a2), (b1, x2)]
            found = lower
        for d, (x1, x2) in enumerate(found):
            self.dx[d, pl.ds(0, self.layers), :] = x1
            self.dx[d, pl.ds(self.layers, self.layers), :] = x2

    def wide(self, ref, index, row):
        rows = [ref[index, pl.ds(row + layer, 1), :] for layer in range(self.layers)]
        return jnp.stack([jnp.broadcast_to(v, (BLOCKS, v.shape[1])) for v in rows])

    def expand(self, phase):
        first, last = self.wide(self.dx, self.me, 0), self.wide(self.dx, self.me, self.layers)
        beyond = self.wide(self.dx, jnp.minimum(self.me + 1, self.count - 1), 0)
        block = sub_index(first.shape)
        for level in reversed(range(len(SHIFTS))):
            shift = SHIFTS[level]
            coef = [self.bcoef[level, c] for c in range(6)]
            a2, b1 = split(first, last, coef, (self.bpart[phase, level, 0], self.bpart[phase, level, 1]))
            odd = lax.rem(block, 2 * shift) == shift
            first = jnp.where(odd, roll(b1, shift), first)
            last = jnp.where(odd, roll(last, shift), a2)
        x = [None] * self.step
        x[0], x[-1] = first, last
        for i, l, r in reversed(self.order):
            x[i] = self.coef[i, 0] * x[l] + self.coef[i, 1] * x[r] + self.part[phase, i]
        after = x[1:] + [jnp.where(block == BLOCKS - 1, beyond, roll(x[0], -1))]
        return x, [now - then for now, then in zip(x, after)]

    def end_a(self):
        self.factor_devices()
        self.solve_devices([(self.dev(d, R1), self.dev(d, R2)) for d in range(self.count)])
        x, change = self.expand(0)
        for k in range(self.step):
            face = self.face[k]
            if k == self.step - 1:
                face = jnp.where(sub_index(face.shape) == BLOCKS - 1, self.wide(self.ends, self.me, 0), face)
            self.flux[k] = -face * change[k]
        return x

    def end_b(self):
        n = self.layers
        self.solve_devices([(self.buf_b[d, pl.ds(0, n), :], self.buf_b[d, pl.ds(n, n), :]) for d in range(self.count)])
        x, change = self.expand(1)
        return x, [self.flux[k] * change[k] for k in range(self.step)]


def kernel(counts, *refs):
    sources_hbm, refs = refs[:9], refs[9:]
    (new_heads, grad_heads, sens_x, sens_y), refs = refs[:4], refs[4:]
    copied, refs = refs[:9], refs[9:]
    heads, cond_x, cond_y, storage, sources, cotangent, mask, scale, window = copied
    (arrive, weight, act, act_t, cond_t, store_t, work, work_t, other_t), rest = refs[:9], refs[9:]
    layers, rows, columns = heads.shape
    half = len(rest) // 2
    x = Direction("gx", counts[0], rows, layers, rest[:half])
    y = Direction("gy", counts[1], columns, layers, rest[half:])
    barrier = pltpu.get_barrier_semaphore()
    x.greet(barrier)
    y.greet(barrier)
    loads = [pltpu.make_async_copy(src, dst, arrive.at[at]) for at, (src, dst) in enumerate(zip(sources_hbm, copied))]
    for at in (8, 7, 6, 1, 3, 0, 4, 2, 5):
        loads[at].start()

    loads[8].wait()
    loads[7].wait()
    for layer in range(layers):
        weight[layer] = jnp.full(weight.shape[1:], scale[window[layer]], jnp.float32)
    loads[6].wait()
    act[...] = mask[...].astype(jnp.float32)
    act_t[...] = act[...].T
    for at in (1, 3, 0, 4):
        loads[at].wait()

    x.begin_a(cond_x, storage, act, weight,
              lambda k: slab(storage, k, x.step) * slab(heads, k, x.step) + slab(sources, k, x.step))
    pl.semaphore_wait(barrier, counts[0] + counts[1] - 2)
    x_a = x.copies(x.buf_a, x.send_a, x.recv_a)
    for copy in x_a:
        copy.start()

    loads[2].wait()
    loads[5].wait()
    for layer in range(layers):
        cond_t[layer] = cond_y[layer].T
        store_t[layer] = storage[layer].T
        work_t[layer] = cotangent[layer].T
    y.begin_a(cond_t, store_t, act_t, weight, lambda k: slab(work_t, k, y.step))
    y_a = y.copies(y.buf_a, y.send_a, y.recv_a)
    for copy in y_a:
        copy.start()

    for copy in x_a:
        copy.wait()
    for k, value in enumerate(x.end_a()):
        put_slab(work, k, x.step, slab(storage, k, x.step) * value)
    for layer in range(layers):
        work_t[layer] = work[layer].T
    y.begin_b(lambda k: slab(work_t, k, y.step))
    y_b = y.copies(y.buf_b, y.send_b, y.recv_b)
    for copy in y_b:
        copy.start()

    for copy in y_a:
        copy.wait()
    for k, value in enumerate(y.end_a()):
        put_slab(other_t, k, y.step, slab(store_t, k, y.step) * value)
    for layer in range(layers):
        work[layer] = other_t[layer].T
    x.begin_b(lambda k: slab(work, k, x.step))
    x_b = x.copies(x.buf_b, x.send_b, x.recv_b)
    for copy in x_b:
        copy.start()

    for copy in y_b:
        copy.wait()
    values, sens = y.end_b()
    for k in range(y.step):
        put_slab(work_t, k, y.step, values[k])
        put_slab(other_t, k, y.step, sens[k])
    for layer in range(layers):
        new_heads[layer] = work_t[layer].T
        sens_y[layer] = other_t[layer].T

    for copy in x_b:
        copy.wait()
    values, sens = x.end_b()
    for k in range(x.step):
        put_slab(grad_heads, k, x.step, slab(storage, k, x.step) * values[k])
        put_slab(sens_x, k, x.step, sens[k])


def write_out(*refs):
    count = len(refs) // 2
    copies = [pltpu.make_async_copy(refs[i], refs[count + i], refs[-1].at[i]) for i in range(count)]
    for copy in copies:
        copy.start()
    for copy in copies:
        copy.wait()


def direction_scratch(count, length, width, layers):
    step = length // BLOCKS
    tile = (layers, BLOCKS, width)
    rows_a = -(-(layers * A + 8) // 8) * 8
    rows_b = -(-(layers * 2) // 8) * 8
    sems = pltpu.SemaphoreType.DMA((max(count - 1, 1),))
    return [
        pltpu.VMEM((step, 3) + tile, jnp.float32),
        pltpu.VMEM((2, step) + tile, jnp.float32),
        pltpu.VMEM((step,) + tile, jnp.float32),
        pltpu.VMEM((step,) + tile, jnp.float32),
        pltpu.VMEM((len(SHIFTS), 6) + tile, jnp.float32),
        pltpu.VMEM((2, len(SHIFTS), 2) + tile, jnp.float32),
        pltpu.VMEM((count, 6, layers, width), jnp.float32),
        pltpu.VMEM((count, rows_b, width), jnp.float32),
        pltpu.VMEM((count, rows_b, width), jnp.float32),
        pltpu.VMEM((count, rows_a, width), jnp.float32),
        pltpu.VMEM((count, rows_b, width), jnp.float32),
        sems, sems, sems, sems,
    ]


def solution(mesh):
    counts = (mesh.shape["gx"], mesh.shape["gy"])

    def on_device(*args):
        layers, rows, columns = args[0].shape
        vmem = pl.BlockSpec(memory_space=pltpu.VMEM)
        hbm = pl.BlockSpec(memory_space=pltpu.HBM)
        natural = pltpu.VMEM((layers, rows, columns), jnp.float32)
        turned = pltpu.VMEM((layers, columns, rows), jnp.float32)
        results = [jax.ShapeDtypeStruct(args[0].shape, jnp.float32)] * 4
        found = pl.pallas_call(
            functools.partial(kernel, counts),
            out_shape=[pltpu.VMEM(args[0].shape, jnp.float32)] * 4,
            in_specs=[hbm] * 9,
            out_specs=[vmem] * 4,
            scratch_shapes=[pltpu.VMEM(v.shape, v.dtype) for v in args[:7]]
            + [pltpu.SMEM(v.shape, v.dtype) for v in args[7:]]
            + [
                pltpu.SemaphoreType.DMA((9,)),
                pltpu.VMEM((layers, BLOCKS, columns), jnp.float32),
                pltpu.VMEM((rows, columns), jnp.float32),
                pltpu.VMEM((columns, rows), jnp.float32),
                turned, turned, natural, turned, turned,
            ]
            + direction_scratch(counts[0], rows, columns, layers)
            + direction_scratch(counts[1], columns, rows, layers),
            compiler_params=pltpu.CompilerParams(
                collective_id=0, has_side_effects=True, vmem_limit_bytes=40 * 2**20
            ),
        )(*[pltpu.with_memory_space_constraint(v, pltpu.HBM) for v in args])
        return pl.pallas_call(
            write_out,
            out_shape=results,
            in_specs=[vmem] * 4,
            out_specs=[hbm] * 4,
            scratch_shapes=[pltpu.SemaphoreType.DMA((4,))],
        )(*found)

    block = P(None, "gx", "gy")
    return jax.shard_map(
        on_device,
        mesh=mesh,
        in_specs=(block,) * 6 + (P("gx", "gy"), P(), P()),
        out_specs=(block,) * 4,
        check_vma=False,
    )
```

```python
import functools

import jax
import jax.numpy as jnp
from jax import lax
from jax.experimental import pallas as pl
from jax.experimental.pallas import tpu as pltpu
from jax.sharding import PartitionSpec as P

MESH = pl.DeviceIdType.MESH
BLOCKS = 8
SHIFTS = (1, 2, 4)
G1, G2, T, R1, R2, F, A = range(7)


def schedule(length):
    alive = list(range(length))
    order = []
    while len(alive) > 2:
        gone = alive[1:-1:2]
        for node in gone:
            at = alive.index(node)
            order.append((node, alive[at - 1], alive[at + 1]))
        alive = [node for node in alive if node not in gone]
    return order


def weights(fl, fr, s):
    inv = 1.0 / (fl + fr + s)
    return fl * inv, fr * inv, inv


def merge(a, b, face):
    g1, g2, t = a
    bg1, bg2, bt = b
    wla, wra, ia = weights(t, face, g2)
    through = t * wra
    gb = bg1 + wra * g2
    wlb, wrb, ib = weights(through, bt, gb)
    return (g1 + wla * g2 + wlb * gb, bg2 + wrb * gb, through * wrb), (wla, wra, ia, wlb, wrb, ib)


def merge_right(a, b, coef):
    wla, wra, ia, wlb, wrb, ib = coef
    r1, r2 = a
    rb = b[0] + wra * r2
    return (r1 + wla * r2 + wlb * rb, b[1] + wrb * rb), (r2 * ia, rb * ib)


def split(x1, x2, coef, parts):
    wla, wra, _, wlb, wrb, _ = coef
    b1 = wlb * x1 + wrb * x2 + parts[1]
    a2 = wla * x1 + wra * b1 + parts[0]
    return a2, b1


def roll(value, shift):
    return pltpu.roll(value, shift % BLOCKS, 1)


def sub_index(shape):
    return lax.broadcasted_iota(jnp.int32, shape, 1)


def slab(ref, k, step):
    return ref[:, pl.ds(k, BLOCKS, stride=step), :]


def put_slab(ref, k, step, value):
    ref[:, pl.ds(k, BLOCKS, stride=step), :] = value


class Direction:
    def __init__(self, axis, count, length, layers, refs):
        self.axis, self.count, self.step, self.layers = axis, count, length // BLOCKS, layers
        (self.coef, self.part, self.face, self.flux, self.store, self.bcoef, self.bpart, self.dcoef, self.dx, self.ends,
         self.buf_a, self.buf_b, self.send_a, self.recv_a, self.send_b, self.recv_b) = refs
        self.me = lax.axis_index(axis)
        self.order = schedule(self.step)

    def peer(self, offset):
        return lax.rem(self.me + offset, self.count)

    def greet(self, barrier):
        for offset in range(1, self.count):
            pl.semaphore_signal(barrier, inc=1, device_id={self.axis: self.peer(offset)}, device_id_type=MESH)

    def copies(self, buf, send, recv):
        return [
            pltpu.make_async_remote_copy(
                src_ref=buf.at[self.me],
                dst_ref=buf.at[self.me],
                send_sem=send.at[offset - 1],
                recv_sem=recv.at[offset - 1],
                device_id={self.axis: self.peer(offset)},
                device_id_type=MESH,
            )
            for offset in range(1, self.count)
        ]

    def reduce_right(self, right, phase):
        for i, l, r in self.order:
            wl, wr, inv = self.coef[i, 0], self.coef[i, 1], self.coef[i, 2]
            right[l] = right[l] + wl * right[i]
            right[r] = right[r] + wr * right[i]
            self.part[phase, i] = right[i] * inv
        pair = (right[0], right[-1])
        for level, shift in enumerate(SHIFTS):
            coef = [self.bcoef[level, c] for c in range(6)]
            pair, parts = merge_right(pair, [roll(v, -shift) for v in pair], coef)
            self.bpart[phase, level, 0], self.bpart[phase, level, 1] = parts
        return pair

    def post(self, buf, at, value, sub=0):
        for layer in range(self.layers):
            buf[self.me, pl.ds(at * self.layers + layer, 1), :] = value[layer, sub : sub + 1, :]

    def begin_a(self, cond, storage, active, weight, right_of):
        step = self.step
        act = [active[pl.ds(k, BLOCKS, stride=step), :] for k in range(step)]
        weight = weight[...]
        store = [slab(storage, k, step) for k in range(step)]
        for k in range(step):
            self.store[k] = store[k]
        right = [right_of(k, store[k]) for k in range(step)]
        face = []
        for k in range(step):
            raw = jnp.exp(slab(cond, k, step)) * weight * act[k][None]
            if k == step - 1:
                self.post(self.buf_a, F, raw, BLOCKS - 1)
                after = pltpu.roll(act[0], BLOCKS - 1, 0)
            else:
                after = act[k + 1]
            face.append(raw * after[None])
            self.face[k] = face[k]
        for i, l, r in self.order:
            wl, wr, inv = weights(face[l], face[i], store[i])
            store[l] = store[l] + wl * store[i]
            store[r] = store[r] + wr * store[i]
            face[l] = face[l] * wr
            self.coef[i, 0], self.coef[i, 1], self.coef[i, 2] = wl, wr, inv
        seg, link = (store[0], store[-1], face[0]), face[-1]
        for level, shift in enumerate(SHIFTS):
            seg, coef = merge(seg, [roll(v, -shift) for v in seg], link)
            link = roll(link, -shift)
            for c in range(6):
                self.bcoef[level, c] = coef[c]
        pair = self.reduce_right(right, 0)
        for at, value in ((G1, seg[0]), (G2, seg[1]), (T, seg[2]), (R1, pair[0]), (R2, pair[1])):
            self.post(self.buf_a, at, value)
        rows = self.layers * A
        self.buf_a[self.me, pl.ds(rows, 8), :] = jnp.broadcast_to(act[0][0:1], (8, act[0].shape[1]))

    def begin_b(self, right_of):
        pair = self.reduce_right([right_of(k) for k in range(self.step)], 1)
        self.post(self.buf_b, 0, pair[0])
        self.post(self.buf_b, 1, pair[1])

    def dev(self, d, at):
        return self.buf_a[d, pl.ds(at * self.layers, self.layers), :]

    def factor_devices(self):
        first_act = [self.buf_a[d, pl.ds(self.layers * A, 1), :] for d in range(self.count)]
        segs = [tuple(self.dev(d, q) for q in (G1, G2, T)) for d in range(self.count)]
        faces = [self.dev(d, F) * first_act[d + 1] for d in range(self.count - 1)] + [jnp.zeros_like(segs[0][0])]
        for d in range(self.count):
            self.ends[d, pl.ds(0, self.layers), :] = faces[d]
        slot = 0
        while len(segs) > 1:
            joined, links = [], []
            for at in range(0, len(segs) - 1, 2):
                seg, coef = merge(segs[at], segs[at + 1], faces[at])
                for c in range(6):
                    self.dcoef[slot, c] = coef[c]
                slot += 1
                joined.append(seg)
                links.append(faces[at + 1])
            if len(segs) % 2:
                joined.append(segs[-1])
                links.append(faces[-1])
            segs, faces = joined, links
        g1, g2, t = segs[0]
        inv = 1.0 / (t + g2)
        w = t * inv
        self.dcoef[slot, 0], self.dcoef[slot, 1], self.dcoef[slot, 2] = w, inv, 1.0 / (g1 + w * g2)

    def solve_devices(self, pairs):
        slot, tree = 0, []
        while len(pairs) > 1:
            joined, record = [], []
            for at in range(0, len(pairs) - 1, 2):
                coef = [self.dcoef[slot, c] for c in range(6)]
                pair, parts = merge_right(pairs[at], pairs[at + 1], coef)
                slot += 1
                joined.append(pair)
                record.append((coef, parts))
            if len(pairs) % 2:
                joined.append(pairs[-1])
                record.append(None)
            pairs = joined
            tree.append(record)
        r1, r2 = pairs[0]
        w, inv, top = (self.dcoef[slot, c] for c in range(3))
        x1 = (r1 + w * r2) * top
        found = [(x1, w * x1 + r2 * inv)]
        for record in reversed(tree):
            lower = []
            for (x1, x2), entry in zip(found, record):
                if entry is None:
                    lower.append((x1, x2))
                else:
                    a2, b1 = split(x1, x2, *entry)
                    lower += [(x1, a2), (b1, x2)]
            found = lower
        for d, (x1, x2) in enumerate(found):
            self.dx[d, pl.ds(0, self.layers), :] = x1
            self.dx[d, pl.ds(self.layers, self.layers), :] = x2

    def wide(self, ref, index, row):
        rows = [ref[index, pl.ds(row + layer, 1), :] for layer in range(self.layers)]
        return jnp.stack([jnp.broadcast_to(v, (BLOCKS, v.shape[1])) for v in rows])

    def expand(self, phase):
        first, last = self.wide(self.dx, self.me, 0), self.wide(self.dx, self.me, self.layers)
        beyond = self.wide(self.dx, jnp.minimum(self.me + 1, self.count - 1), 0)
        block = sub_index(first.shape)
        for level in reversed(range(len(SHIFTS))):
            shift = SHIFTS[level]
            coef = [self.bcoef[level, c] for c in range(6)]
            a2, b1 = split(first, last, coef, (self.bpart[phase, level, 0], self.bpart[phase, level, 1]))
            odd = lax.rem(block, 2 * shift) == shift
            first = jnp.where(odd, roll(b1, shift), first)
            last = jnp.where(odd, roll(last, shift), a2)
        x = [None] * self.step
        x[0], x[-1] = first, last
        for i, l, r in reversed(self.order):
            x[i] = self.coef[i, 0] * x[l] + self.coef[i, 1] * x[r] + self.part[phase, i]
        after = x[1:] + [jnp.where(block == BLOCKS - 1, beyond, roll(x[0], -1))]
        return x, [now - then for now, then in zip(x, after)]

    def end_a(self):
        self.factor_devices()
        self.solve_devices([(self.dev(d, R1), self.dev(d, R2)) for d in range(self.count)])
        x, change = self.expand(0)
        for k in range(self.step):
            face = self.face[k]
            if k == self.step - 1:
                face = jnp.where(sub_index(face.shape) == BLOCKS - 1, self.wide(self.ends, self.me, 0), face)
            self.flux[k] = -face * change[k]
        return x

    def end_b(self):
        n = self.layers
        self.solve_devices([(self.buf_b[d, pl.ds(0, n), :], self.buf_b[d, pl.ds(n, n), :]) for d in range(self.count)])
        x, change = self.expand(1)
        return x, [self.flux[k] * change[k] for k in range(self.step)]


def kernel(counts, *refs):
    sources_hbm, refs = refs[:9], refs[9:]
    (new_heads, grad_heads, sens_x, sens_y), refs = refs[:4], refs[4:]
    copied, refs = refs[:9], refs[9:]
    heads, cond_x, cond_y, storage, sources, cotangent, mask, scale, window = copied
    (arrive, weight, act, act_t, cond_t, store_t, work, work_t, other_t), rest = refs[:9], refs[9:]
    layers, rows, columns = heads.shape
    half = len(rest) // 2
    x = Direction("gx", counts[0], rows, layers, rest[:half])
    y = Direction("gy", counts[1], columns, layers, rest[half:])
    barrier = pltpu.get_barrier_semaphore()
    x.greet(barrier)
    y.greet(barrier)
    loads = [pltpu.make_async_copy(src, dst, arrive.at[at]) for at, (src, dst) in enumerate(zip(sources_hbm, copied))]
    for at in (8, 7, 6, 1, 3, 0, 4, 2, 5):
        loads[at].start()

    loads[8].wait()
    loads[7].wait()
    for layer in range(layers):
        weight[layer] = jnp.full(weight.shape[1:], scale[window[layer]], jnp.float32)
    loads[6].wait()
    act[...] = mask[...].astype(jnp.float32)
    act_t[...] = act[...].T
    for at in (1, 3, 0, 4):
        loads[at].wait()

    x.begin_a(cond_x, storage, act, weight,
              lambda k, store: store * slab(heads, k, x.step) + slab(sources, k, x.step))
    pl.semaphore_wait(barrier, counts[0] + counts[1] - 2)
    x_a = x.copies(x.buf_a, x.send_a, x.recv_a)
    for copy in x_a:
        copy.start()

    loads[2].wait()
    loads[5].wait()
    for layer in range(layers):
        cond_t[layer] = cond_y[layer].T
        store_t[layer] = storage[layer].T
        work_t[layer] = cotangent[layer].T
    y.begin_a(cond_t, store_t, act_t, weight, lambda k, store: slab(work_t, k, y.step))
    y_a = y.copies(y.buf_a, y.send_a, y.recv_a)
    for copy in y_a:
        copy.start()

    for copy in x_a:
        copy.wait_recv()
    for k, value in enumerate(x.end_a()):
        put_slab(work, k, x.step, x.store[k] * value)
    for layer in range(layers):
        work_t[layer] = work[layer].T
    y.begin_b(lambda k: slab(work_t, k, y.step))
    y_b = y.copies(y.buf_b, y.send_b, y.recv_b)
    for copy in y_b:
        copy.start()

    for copy in y_a:
        copy.wait_recv()
    for k, value in enumerate(y.end_a()):
        put_slab(other_t, k, y.step, y.store[k] * value)
    for layer in range(layers):
        work[layer] = other_t[layer].T
    x.begin_b(lambda k: slab(work, k, x.step))
    x_b = x.copies(x.buf_b, x.send_b, x.recv_b)
    for copy in x_b:
        copy.start()

    for copy in y_b:
        copy.wait_recv()
    values, sens = y.end_b()
    for k in range(y.step):
        put_slab(work_t, k, y.step, values[k])
        put_slab(other_t, k, y.step, sens[k])
    for layer in range(layers):
        new_heads[layer] = work_t[layer].T
        sens_y[layer] = other_t[layer].T

    for copy in x_b:
        copy.wait_recv()
    values, sens = x.end_b()
    for k in range(x.step):
        put_slab(grad_heads, k, x.step, x.store[k] * values[k])
        put_slab(sens_x, k, x.step, sens[k])
    for copy in x_a + y_a + x_b + y_b:
        copy.wait_send()


def write_out(*refs):
    count = len(refs) // 2
    copies = [pltpu.make_async_copy(refs[i], refs[count + i], refs[-1].at[i]) for i in range(count)]
    for copy in copies:
        copy.start()
    for copy in copies:
        copy.wait()


def direction_scratch(count, length, width, layers):
    step = length // BLOCKS
    tile = (layers, BLOCKS, width)
    rows_a = -(-(layers * A + 8) // 8) * 8
    rows_b = -(-(layers * 2) // 8) * 8
    sems = pltpu.SemaphoreType.DMA((max(count - 1, 1),))
    return [
        pltpu.VMEM((step, 3) + tile, jnp.float32),
        pltpu.VMEM((2, step) + tile, jnp.float32),
        pltpu.VMEM((step,) + tile, jnp.float32),
        pltpu.VMEM((step,) + tile, jnp.float32),
        pltpu.VMEM((step,) + tile, jnp.float32),
        pltpu.VMEM((len(SHIFTS), 6) + tile, jnp.float32),
        pltpu.VMEM((2, len(SHIFTS), 2) + tile, jnp.float32),
        pltpu.VMEM((count, 6, layers, width), jnp.float32),
        pltpu.VMEM((count, rows_b, width), jnp.float32),
        pltpu.VMEM((count, rows_b, width), jnp.float32),
        pltpu.VMEM((count, rows_a, width), jnp.float32),
        pltpu.VMEM((count, rows_b, width), jnp.float32),
        sems, sems, sems, sems,
    ]


def solution(mesh):
    counts = (mesh.shape["gx"], mesh.shape["gy"])

    def on_device(*args):
        layers, rows, columns = args[0].shape
        vmem = pl.BlockSpec(memory_space=pltpu.VMEM)
        hbm = pl.BlockSpec(memory_space=pltpu.HBM)
        natural = pltpu.VMEM((layers, rows, columns), jnp.float32)
        turned = pltpu.VMEM((layers, columns, rows), jnp.float32)
        results = [jax.ShapeDtypeStruct(args[0].shape, jnp.float32)] * 4
        found = pl.pallas_call(
            functools.partial(kernel, counts),
            out_shape=[pltpu.VMEM(args[0].shape, jnp.float32)] * 4,
            in_specs=[hbm] * 9,
            out_specs=[vmem] * 4,
            scratch_shapes=[pltpu.VMEM(v.shape, v.dtype) for v in args[:7]]
            + [pltpu.SMEM(v.shape, v.dtype) for v in args[7:]]
            + [
                pltpu.SemaphoreType.DMA((9,)),
                pltpu.VMEM((layers, BLOCKS, columns), jnp.float32),
                pltpu.VMEM((rows, columns), jnp.float32),
                pltpu.VMEM((columns, rows), jnp.float32),
                turned, turned, natural, turned, turned,
            ]
            + direction_scratch(counts[0], rows, columns, layers)
            + direction_scratch(counts[1], columns, rows, layers),
            compiler_params=pltpu.CompilerParams(
                collective_id=0, has_side_effects=True, vmem_limit_bytes=40 * 2**20
            ),
        )(*[pltpu.with_memory_space_constraint(v, pltpu.HBM) for v in args])
        return pl.pallas_call(
            write_out,
            out_shape=results,
            in_specs=[vmem] * 4,
            out_specs=[hbm] * 4,
            scratch_shapes=[pltpu.SemaphoreType.DMA((4,))],
            compiler_params=pltpu.CompilerParams(vmem_limit_bytes=2 * 2**20),
        )(*[pltpu.with_memory_space_constraint(v, pltpu.VMEM) for v in found])

    block = P(None, "gx", "gy")
    return jax.shard_map(
        on_device,
        mesh=mesh,
        in_specs=(block,) * 6 + (P("gx", "gy"), P(), P()),
        out_specs=(block,) * 4,
        check_vma=False,
    )
```

```python
import functools

import jax
import jax.numpy as jnp
from jax import lax
from jax.experimental import pallas as pl
from jax.experimental.pallas import tpu as pltpu
from jax.sharding import PartitionSpec as P

MESH = pl.DeviceIdType.MESH
BLOCKS = 8
SHIFTS = (1, 2, 4)
G1, G2, T, R1, R2, F, A = range(7)


def schedule(length):
    alive = list(range(length))
    order = []
    while len(alive) > 2:
        gone = alive[1:-1:2]
        for node in gone:
            at = alive.index(node)
            order.append((node, alive[at - 1], alive[at + 1]))
        alive = [node for node in alive if node not in gone]
    return order


def weights(fl, fr, s):
    inv = pl.reciprocal(fl + fr + s)
    return fl * inv, fr * inv, inv


def merge(a, b, face):
    g1, g2, t = a
    bg1, bg2, bt = b
    wla, wra, ia = weights(t, face, g2)
    through = t * wra
    gb = bg1 + wra * g2
    wlb, wrb, ib = weights(through, bt, gb)
    return (g1 + wla * g2 + wlb * gb, bg2 + wrb * gb, through * wrb), (wla, wra, ia, wlb, wrb, ib)


def merge_right(a, b, coef):
    wla, wra, ia, wlb, wrb, ib = coef
    r1, r2 = a
    rb = b[0] + wra * r2
    return (r1 + wla * r2 + wlb * rb, b[1] + wrb * rb), (r2 * ia, rb * ib)


def split(x1, x2, coef, parts):
    wla, wra, _, wlb, wrb, _ = coef
    b1 = wlb * x1 + wrb * x2 + parts[1]
    a2 = wla * x1 + wra * b1 + parts[0]
    return a2, b1


def roll(value, shift):
    return pltpu.roll(value, shift % BLOCKS, 1)


def sub_index(shape):
    return lax.broadcasted_iota(jnp.int32, shape, 1)


def slab(ref, k, step):
    return ref[:, pl.ds(k, BLOCKS, stride=step), :]


def put_slab(ref, k, step, value):
    ref[:, pl.ds(k, BLOCKS, stride=step), :] = value


class Direction:
    def __init__(self, axis, count, length, layers, refs):
        self.axis, self.count, self.step, self.layers = axis, count, length // BLOCKS, layers
        (self.coef, self.part, self.face, self.flux, self.store, self.bcoef, self.bpart, self.dcoef, self.dx, self.ends,
         self.buf_a, self.buf_b, self.send_a, self.recv_a, self.send_b, self.recv_b) = refs
        self.me = lax.axis_index(axis)
        self.order = schedule(self.step)

    def peer(self, offset):
        return lax.rem(self.me + offset, self.count)

    def greet(self, barrier):
        for offset in range(1, self.count):
            pl.semaphore_signal(barrier, inc=1, device_id={self.axis: self.peer(offset)}, device_id_type=MESH)

    def copies(self, buf, send, recv):
        return [
            pltpu.make_async_remote_copy(
                src_ref=buf.at[self.me],
                dst_ref=buf.at[self.me],
                send_sem=send.at[offset - 1],
                recv_sem=recv.at[offset - 1],
                device_id={self.axis: self.peer(offset)},
                device_id_type=MESH,
            )
            for offset in range(1, self.count)
        ]

    def reduce_right(self, right, phase):
        for i, l, r in self.order:
            wl, wr, inv = self.coef[i, 0], self.coef[i, 1], self.coef[i, 2]
            right[l] = right[l] + wl * right[i]
            right[r] = right[r] + wr * right[i]
            self.part[phase, i] = right[i] * inv
        pair = (right[0], right[-1])
        for level, shift in enumerate(SHIFTS):
            coef = [self.bcoef[level, c] for c in range(6)]
            pair, parts = merge_right(pair, [roll(v, -shift) for v in pair], coef)
            self.bpart[phase, level, 0], self.bpart[phase, level, 1] = parts
        return pair

    def post(self, buf, at, value, sub=0):
        for layer in range(self.layers):
            buf[self.me, pl.ds(at * self.layers + layer, 1), :] = value[layer, sub : sub + 1, :]

    def begin_a(self, cond, storage, active, weight, right_of):
        step = self.step
        act = [active[pl.ds(k, BLOCKS, stride=step), :] for k in range(step)]
        weight = weight[...]
        store = [slab(storage, k, step) for k in range(step)]
        for k in range(step):
            self.store[k] = store[k]
        right = [right_of(k, store[k]) for k in range(step)]
        face = []
        for k in range(step):
            raw = jnp.exp(slab(cond, k, step)) * weight * act[k][None]
            if k == step - 1:
                self.post(self.buf_a, F, raw, BLOCKS - 1)
                after = pltpu.roll(act[0], BLOCKS - 1, 0)
            else:
                after = act[k + 1]
            face.append(raw * after[None])
            self.face[k] = face[k]
        for i, l, r in self.order:
            wl, wr, inv = weights(face[l], face[i], store[i])
            store[l] = store[l] + wl * store[i]
            store[r] = store[r] + wr * store[i]
            face[l] = face[l] * wr
            self.coef[i, 0], self.coef[i, 1], self.coef[i, 2] = wl, wr, inv
        seg, link = (store[0], store[-1], face[0]), face[-1]
        for level, shift in enumerate(SHIFTS):
            seg, coef = merge(seg, [roll(v, -shift) for v in seg], link)
            link = roll(link, -shift)
            for c in range(6):
                self.bcoef[level, c] = coef[c]
        pair = self.reduce_right(right, 0)
        for at, value in ((G1, seg[0]), (G2, seg[1]), (T, seg[2]), (R1, pair[0]), (R2, pair[1])):
            self.post(self.buf_a, at, value)
        rows = self.layers * A
        self.buf_a[self.me, pl.ds(rows, 8), :] = jnp.broadcast_to(act[0][0:1], (8, act[0].shape[1]))

    def begin_b(self, right_of):
        pair = self.reduce_right([right_of(k) for k in range(self.step)], 1)
        self.post(self.buf_b, 0, pair[0])
        self.post(self.buf_b, 1, pair[1])

    def dev(self, d, at):
        return self.buf_a[d, pl.ds(at * self.layers, self.layers), :]

    def factor_devices(self):
        first_act = [self.buf_a[d, pl.ds(self.layers * A, 1), :] for d in range(self.count)]
        segs = [tuple(self.dev(d, q) for q in (G1, G2, T)) for d in range(self.count)]
        faces = [self.dev(d, F) * first_act[d + 1] for d in range(self.count - 1)] + [jnp.zeros_like(segs[0][0])]
        for d in range(self.count):
            self.ends[d, pl.ds(0, self.layers), :] = faces[d]
        slot = 0
        while len(segs) > 1:
            joined, links = [], []
            for at in range(0, len(segs) - 1, 2):
                seg, coef = merge(segs[at], segs[at + 1], faces[at])
                for c in range(6):
                    self.dcoef[slot, c] = coef[c]
                slot += 1
                joined.append(seg)
                links.append(faces[at + 1])
            if len(segs) % 2:
                joined.append(segs[-1])
                links.append(faces[-1])
            segs, faces = joined, links
        g1, g2, t = segs[0]
        inv = pl.reciprocal(t + g2)
        w = t * inv
        self.dcoef[slot, 0], self.dcoef[slot, 1], self.dcoef[slot, 2] = w, inv, pl.reciprocal(g1 + w * g2)

    def solve_devices(self, pairs):
        slot, tree = 0, []
        while len(pairs) > 1:
            joined, record = [], []
            for at in range(0, len(pairs) - 1, 2):
                coef = [self.dcoef[slot, c] for c in range(6)]
                pair, parts = merge_right(pairs[at], pairs[at + 1], coef)
                slot += 1
                joined.append(pair)
                record.append((coef, parts))
            if len(pairs) % 2:
                joined.append(pairs[-1])
                record.append(None)
            pairs = joined
            tree.append(record)
        r1, r2 = pairs[0]
        w, inv, top = (self.dcoef[slot, c] for c in range(3))
        x1 = (r1 + w * r2) * top
        found = [(x1, w * x1 + r2 * inv)]
        for record in reversed(tree):
            lower = []
            for (x1, x2), entry in zip(found, record):
                if entry is None:
                    lower.append((x1, x2))
                else:
                    a2, b1 = split(x1, x2, *entry)
                    lower += [(x1, a2), (b1, x2)]
            found = lower
        for d, (x1, x2) in enumerate(found):
            self.dx[d, pl.ds(0, self.layers), :] = x1
            self.dx[d, pl.ds(self.layers, self.layers), :] = x2

    def wide(self, ref, index, row):
        rows = [ref[index, pl.ds(row + layer, 1), :] for layer in range(self.layers)]
        return jnp.stack([jnp.broadcast_to(v, (BLOCKS, v.shape[1])) for v in rows])

    def expand(self, phase):
        first, last = self.wide(self.dx, self.me, 0), self.wide(self.dx, self.me, self.layers)
        beyond = self.wide(self.dx, jnp.minimum(self.me + 1, self.count - 1), 0)
        block = sub_index(first.shape)
        for level in reversed(range(len(SHIFTS))):
            shift = SHIFTS[level]
            coef = [self.bcoef[level, c] for c in range(6)]
            a2, b1 = split(first, last, coef, (self.bpart[phase, level, 0], self.bpart[phase, level, 1]))
            odd = lax.rem(block, 2 * shift) == shift
            first = jnp.where(odd, roll(b1, shift), first)
            last = jnp.where(odd, roll(last, shift), a2)
        x = [None] * self.step
        x[0], x[-1] = first, last
        for i, l, r in reversed(self.order):
            x[i] = self.coef[i, 0] * x[l] + self.coef[i, 1] * x[r] + self.part[phase, i]
        after = x[1:] + [jnp.where(block == BLOCKS - 1, beyond, roll(x[0], -1))]
        return x, [now - then for now, then in zip(x, after)]

    def end_a(self):
        self.factor_devices()
        self.solve_devices([(self.dev(d, R1), self.dev(d, R2)) for d in range(self.count)])
        x, change = self.expand(0)
        for k in range(self.step):
            face = self.face[k]
            if k == self.step - 1:
                face = jnp.where(sub_index(face.shape) == BLOCKS - 1, self.wide(self.ends, self.me, 0), face)
            self.flux[k] = -face * change[k]
        return x

    def end_b(self):
        n = self.layers
        self.solve_devices([(self.buf_b[d, pl.ds(0, n), :], self.buf_b[d, pl.ds(n, n), :]) for d in range(self.count)])
        x, change = self.expand(1)
        return x, [self.flux[k] * change[k] for k in range(self.step)]


def kernel(counts, *refs):
    sources_hbm, refs = refs[:9], refs[9:]
    (new_heads, grad_heads, sens_x, sens_y), refs = refs[:4], refs[4:]
    copied, refs = refs[:9], refs[9:]
    heads, cond_x, cond_y, storage, sources, cotangent, mask, scale, window = copied
    (arrive, weight, act, act_t, cond_t, store_t, work, work_t, other_t), rest = refs[:9], refs[9:]
    layers, rows, columns = heads.shape
    half = len(rest) // 2
    x = Direction("gx", counts[0], rows, layers, rest[:half])
    y = Direction("gy", counts[1], columns, layers, rest[half:])
    barrier = pltpu.get_barrier_semaphore()
    x.greet(barrier)
    y.greet(barrier)
    loads = [pltpu.make_async_copy(src, dst, arrive.at[at]) for at, (src, dst) in enumerate(zip(sources_hbm, copied))]
    for at in (8, 7, 6, 1, 3, 0, 4, 2, 5):
        loads[at].start()

    loads[8].wait()
    loads[7].wait()
    for layer in range(layers):
        weight[layer] = jnp.full(weight.shape[1:], scale[window[layer]], jnp.float32)
    loads[6].wait()
    act[...] = mask[...].astype(jnp.float32)
    act_t[...] = act[...].T
    for at in (1, 3, 0, 4):
        loads[at].wait()

    x.begin_a(cond_x, storage, act, weight,
              lambda k, store: store * slab(heads, k, x.step) + slab(sources, k, x.step))
    pl.semaphore_wait(barrier, counts[0] + counts[1] - 2)
    x_a = x.copies(x.buf_a, x.send_a, x.recv_a)
    for copy in x_a:
        copy.start()

    loads[2].wait()
    loads[5].wait()
    for layer in range(layers):
        cond_t[layer] = cond_y[layer].T
        store_t[layer] = storage[layer].T
        work_t[layer] = cotangent[layer].T
    y.begin_a(cond_t, store_t, act_t, weight, lambda k, store: slab(work_t, k, y.step))
    y_a = y.copies(y.buf_a, y.send_a, y.recv_a)
    for copy in y_a:
        copy.start()

    for copy in x_a:
        copy.wait_recv()
    for k, value in enumerate(x.end_a()):
        put_slab(work, k, x.step, x.store[k] * value)
    for layer in range(layers):
        work_t[layer] = work[layer].T
    y.begin_b(lambda k: slab(work_t, k, y.step))
    y_b = y.copies(y.buf_b, y.send_b, y.recv_b)
    for copy in y_b:
        copy.start()

    for copy in y_a:
        copy.wait_recv()
    for k, value in enumerate(y.end_a()):
        put_slab(other_t, k, y.step, y.store[k] * value)
    for layer in range(layers):
        work[layer] = other_t[layer].T
    x.begin_b(lambda k: slab(work, k, x.step))
    x_b = x.copies(x.buf_b, x.send_b, x.recv_b)
    for copy in x_b:
        copy.start()

    for copy in y_b:
        copy.wait_recv()
    values, sens = y.end_b()
    for k in range(y.step):
        put_slab(work_t, k, y.step, values[k])
        put_slab(other_t, k, y.step, sens[k])
    for layer in range(layers):
        new_heads[layer] = work_t[layer].T
        sens_y[layer] = other_t[layer].T

    for copy in x_b:
        copy.wait_recv()
    values, sens = x.end_b()
    for k in range(x.step):
        put_slab(grad_heads, k, x.step, x.store[k] * values[k])
        put_slab(sens_x, k, x.step, sens[k])
    for copy in x_a + y_a + x_b + y_b:
        copy.wait_send()


def write_out(*refs):
    count = len(refs) // 2
    copies = [pltpu.make_async_copy(refs[i], refs[count + i], refs[-1].at[i]) for i in range(count)]
    for copy in copies:
        copy.start()
    for copy in copies:
        copy.wait()


def direction_scratch(count, length, width, layers):
    step = length // BLOCKS
    tile = (layers, BLOCKS, width)
    rows_a = -(-(layers * A + 8) // 8) * 8
    rows_b = -(-(layers * 2) // 8) * 8
    sems = pltpu.SemaphoreType.DMA((max(count - 1, 1),))
    return [
        pltpu.VMEM((step, 3) + tile, jnp.float32),
        pltpu.VMEM((2, step) + tile, jnp.float32),
        pltpu.VMEM((step,) + tile, jnp.float32),
        pltpu.VMEM((step,) + tile, jnp.float32),
        pltpu.VMEM((step,) + tile, jnp.float32),
        pltpu.VMEM((len(SHIFTS), 6) + tile, jnp.float32),
        pltpu.VMEM((2, len(SHIFTS), 2) + tile, jnp.float32),
        pltpu.VMEM((count, 6, layers, width), jnp.float32),
        pltpu.VMEM((count, rows_b, width), jnp.float32),
        pltpu.VMEM((count, rows_b, width), jnp.float32),
        pltpu.VMEM((count, rows_a, width), jnp.float32),
        pltpu.VMEM((count, rows_b, width), jnp.float32),
        sems, sems, sems, sems,
    ]


def solution(mesh):
    counts = (mesh.shape["gx"], mesh.shape["gy"])

    def on_device(*args):
        layers, rows, columns = args[0].shape
        vmem = pl.BlockSpec(memory_space=pltpu.VMEM)
        hbm = pl.BlockSpec(memory_space=pltpu.HBM)
        natural = pltpu.VMEM((layers, rows, columns), jnp.float32)
        turned = pltpu.VMEM((layers, columns, rows), jnp.float32)
        results = [jax.ShapeDtypeStruct(args[0].shape, jnp.float32)] * 4
        found = pl.pallas_call(
            functools.partial(kernel, counts),
            out_shape=[pltpu.VMEM(args[0].shape, jnp.float32)] * 4,
            in_specs=[hbm] * 9,
            out_specs=[vmem] * 4,
            scratch_shapes=[pltpu.VMEM(v.shape, v.dtype) for v in args[:7]]
            + [pltpu.SMEM(v.shape, v.dtype) for v in args[7:]]
            + [
                pltpu.SemaphoreType.DMA((9,)),
                pltpu.VMEM((layers, BLOCKS, columns), jnp.float32),
                pltpu.VMEM((rows, columns), jnp.float32),
                pltpu.VMEM((columns, rows), jnp.float32),
                turned, turned, natural, turned, turned,
            ]
            + direction_scratch(counts[0], rows, columns, layers)
            + direction_scratch(counts[1], columns, rows, layers),
            compiler_params=pltpu.CompilerParams(
                collective_id=0, has_side_effects=True, vmem_limit_bytes=40 * 2**20
            ),
        )(*[pltpu.with_memory_space_constraint(v, pltpu.HBM) for v in args])
        return pl.pallas_call(
            write_out,
            out_shape=results,
            in_specs=[vmem] * 4,
            out_specs=[hbm] * 4,
            scratch_shapes=[pltpu.SemaphoreType.DMA((4,))],
            compiler_params=pltpu.CompilerParams(vmem_limit_bytes=2 * 2**20),
        )(*[pltpu.with_memory_space_constraint(v, pltpu.VMEM) for v in found])

    block = P(None, "gx", "gy")
    return jax.shard_map(
        on_device,
        mesh=mesh,
        in_specs=(block,) * 6 + (P("gx", "gy"), P(), P()),
        out_specs=(block,) * 4,
        check_vma=False,
    )
```
